32 devices in a mesh: row: 4 (over x, core), col: 4 (over z), layer: 2 (over y).
Axes of the slice: x: 2, y: 2, z: 4, core: 2. Of those that a mesh axis runs over, the one named last changes fastest.
Arguments:
- a_vals: bfloat16 [4, 4, 2, 24, 128, 128], P('row', 'col', 'layer'), may hold values from -1.1953125 to 1.1953125
- a_pos: int32 [4, 4, 2, 24], P('row', 'col', 'layer'), may hold values from 0 to 31, as said below
- a_count: int32 [4, 4, 2], P('row', 'col', 'layer'), may hold values from 6 to 24
- b_vals: bfloat16 [4, 4, 2, 1, 6, 128, 128], P('row', 'col', 'layer'), may hold values from -1.1953125 to 1.1953125
- b_pos: int32 [4, 4, 2, 1, 6], P('row', 'col', 'layer'), may hold values from 0 to 31, as said below
- b_count: int32 [4, 4, 2, 1], P('row', 'col', 'layer'), may hold values from 1 to 6
Outputs:
- product: float32 [4096, 4096], P('row', ('col', 'layer'))
The draws below stay inside these ranges and needn't reach their ends.
Inputs may be any that keep to these rules, and one draw needn't show every extreme that they name: `a_pos`: within one panel (fixed first three indices) the 24 entries are distinct. `b_pos`: within one panel (fixed first four indices) the 6 entries are distinct.
All inputs are finite; a program needn't handle non-finite values.
Results may differ from the reference program's by a relative error of at most 0.0003.
Values may be sent and summed in bfloat16 or wider, within the bound.
A program may use at most 64 MiB of HBM per device.

```python
import jax
import jax.numpy as jnp
from jax import lax

BLOCK = 128
KB = 4
CB = 8
RB = 8
SB = 6
SA = 24
PR = 4
PC = 4
PL = 2
HB = 1
NR = 32
NC = 32


def first_slots(key, panels, span, keep):
    keys = jax.random.split(key, panels)
    orders = jax.vmap(lambda one: jax.random.permutation(one, span))(keys)
    return orders[:, :keep].astype(jnp.int32)


def filled_counts(key, panels, lowest, most):
    first, second = jax.random.split(key)
    counts = jax.random.randint(first, (panels,), lowest, most + 1, dtype=jnp.int32)
    where = jax.random.randint(second, (), 0, panels, dtype=jnp.int32)
    return counts.at[where].set(most)


def draw_a_pos(key, part):
    key = jax.random.fold_in(key, 11)
    slots = first_slots(key, PR * PC * PL, RB * KB, SA)
    return slots.reshape(PR, PC, PL, SA)


def draw_a_count(key, part):
    key = jax.random.fold_in(key, 12)
    counts = filled_counts(key, PR * PC * PL, max(SA // 4, 1), SA)
    return counts.reshape(PR, PC, PL)


def draw_b_pos(key, part):
    key = jax.random.fold_in(key, 13)
    slots = first_slots(key, PR * PC * PL * HB, KB * CB, SB)
    return slots.reshape(PR, PC, PL, HB, SB)


def draw_b_count(key, part):
    key = jax.random.fold_in(key, 14)
    counts = filled_counts(key, PR * PC * PL * HB, 1, SB)
    return counts.reshape(PR, PC, PL, HB)


def level_of(rng, dims, pieces, least, top_value):
    def one(dim, shards_of):
        steps = jax.random.uniform(jax.random.fold_in(jax.random.fold_in(rng, 6), dim), (shards_of,), jnp.float32, least / len(pieces), top_value / len(pieces))
        return jnp.repeat(jnp.exp(steps), dims[dim] // shards_of).reshape((-1,) + (1,) * (len(dims) - dim - 1))

    gain = one(*pieces[0])
    for cut in pieces[1:]:
        gain = gain * one(*cut)
    return gain


def gaussian(rng, extent, scale, limit, cuts=(), held_as=jnp.bfloat16):
    level = level_of(rng, extent, cuts, -0.22, 0.18) if cuts else 1.0
    entries = jax.random.normal(rng, extent, jnp.float32) * scale * level
    return jnp.minimum(jnp.maximum(entries, -limit), limit).astype(held_as)


def setup_inputs(seed: int = 0) -> dict:
    key_list = jax.random.split(jax.random.key(seed), 7)
    a_vals = gaussian(key_list[0], (PR, PC, PL, SA, BLOCK, BLOCK), 0.2, 1.1953125, ((0, 4), (1, 4), (2, 2)))
    a_pos = draw_a_pos(jax.random.fold_in(key_list[6], 71), 0)
    a_count = draw_a_count(jax.random.fold_in(key_list[6], 71), 0)
    b_vals = gaussian(key_list[3], (PR, PC, PL, HB, SB, BLOCK, BLOCK), 0.2, 1.1953125, ((0, 4), (1, 4), (2, 2)))
    b_pos = draw_b_pos(jax.random.fold_in(key_list[6], 71), 0)
    b_count = draw_b_count(jax.random.fold_in(key_list[6], 71), 0)
    return {"a_vals": a_vals, "a_pos": a_pos, "a_count": a_count, "b_vals": b_vals, "b_pos": b_pos, "b_count": b_count}


def contribute(total, a_vals, a_pos, a_count, b_vals, b_pos, b_count):
    block = a_vals.shape[-1]
    slots_a = a_vals.shape[0]
    target = (a_pos % KB) * RB + a_pos // KB
    live_a = jnp.arange(slots_a, dtype=jnp.int32) < a_count
    places = jnp.arange(KB * RB, dtype=jnp.int32)
    select = ((target[:, None] == places[None, :]) & live_a[:, None]).astype(jnp.float32)
    placed = jnp.einsum("sp,sab->pab", select, a_vals.astype(jnp.float32)).astype(jnp.bfloat16)
    columns = placed.reshape(KB, RB * block, block)
    for slot in range(b_vals.shape[0]):
        entry = b_pos[slot]
        left = lax.dynamic_index_in_dim(columns, entry // CB, 0, keepdims=False)
        term = jnp.dot(left, b_vals[slot], preferred_element_type=jnp.float32)
        live = (slot < b_count).astype(jnp.float32)
        start = (entry % CB) * block
        old = lax.dynamic_slice_in_dim(total, start, block, 1)
        total = lax.dynamic_update_slice_in_dim(total, old + live * term, start, 1)
    return total


def reference(a_vals, a_pos, a_count, b_vals, b_pos, b_count):
    height = RB * BLOCK
    breadth = CB * BLOCK

    def one_panel(index):
        row_i = index // PC
        col_j = index % PC

        def one_turn(total, turn):
            group = turn // PC
            local = turn % PC
            a_col = (local - row_i) % PC
            b_row = (local - col_j) % PR
            stack = local // PR
            total = contribute(total, a_vals[row_i, a_col, group], a_pos[row_i, a_col, group],
                               a_count[row_i, a_col, group], b_vals[b_row, col_j, group, stack],
                               b_pos[b_row, col_j, group, stack], b_count[b_row, col_j, group, stack])
            return total, None

        start = jnp.zeros((height, breadth), jnp.float32)
        total, _ = lax.scan(one_turn, start, jnp.arange(PL * PC, dtype=jnp.int32))
        return total

    panels = lax.map(one_panel, jnp.arange(PR * PC, dtype=jnp.int32))
    panels = panels.reshape(PR, PC, height, breadth).transpose(0, 2, 1, 3)
    return panels.reshape(NR * BLOCK, NC * BLOCK)
```

```python
import functools

import jax
import jax.numpy as jnp
from jax import lax
from jax.experimental import pallas as pl
from jax.experimental.pallas import tpu as pltpu
from jax.sharding import PartitionSpec as P

KB = 4
CB = 8
RB = 8
MESH = pl.DeviceIdType.MESH


def gather_kernel(
    n_row, n_col, n_layer, pieces,
    a_ref, am_ref, b_ref, bm_ref,
    a_all, am_all, b_all, bm_all,
    up_sem, down_sem, over_sem, a_recv, am_send, am_recv,
    b_send, b_pass, b_recv, bm_send, bm_recv, own_sem,
):
    i = lax.axis_index("row")
    c = lax.axis_index("col")
    l = lax.axis_index("layer")
    m = 1 - l
    size = a_ref.shape[0] // pieces
    half = pieces // 2
    short_cuts = n_col >= 4

    peers = []
    for dl in range(n_layer):
        ll = lax.rem(l + dl, n_layer)
        for dc in range(n_col):
            if dl or dc:
                peers.append((i, lax.rem(c + dc, n_col), ll))
    sides = []
    for dl in range(n_layer):
        ll = lax.rem(l + dl, n_layer)
        for dr in range(n_row):
            if dl or dr:
                sides.append((lax.rem(i + dr, n_row), c, ll))
    greeted = peers + [s for k, s in enumerate(sides) if (k + 1) % n_row != 0]

    barrier = pltpu.get_barrier_semaphore()
    for one in greeted:
        pl.semaphore_signal(barrier, inc=1, device_id=one, device_id_type=MESH)
    pl.semaphore_wait(barrier, len(greeted))

    sent = []

    def send(src, dst, s_sem, r_sem, to, when=None):
        def copy():
            return pltpu.make_async_remote_copy(
                src_ref=src, dst_ref=dst, send_sem=s_sem, recv_sem=r_sem,
                device_id=to, device_id_type=MESH)

        if when is None:
            copy().start()
        else:
            pl.when(when)(lambda: copy().start())
        sent.append((copy, when))

    def arrived(dst, r_sem):
        pltpu.make_async_copy(dst, dst, r_sem).wait()

    def piece(layer, col, q):
        return a_all.at[layer, col, pl.ds(q * size, size)]

    for k, one in enumerate(peers):
        send(am_ref, am_all.at[l, c], am_send.at[k], am_recv.at[l, c], one)
    for k, one in enumerate(sides):
        send(bm_ref, bm_all.at[l, i], bm_send.at[k], bm_recv.at[l, i], one)

    send(b_ref, b_all.at[l, i], b_send.at[0], b_recv.at[l, i], (i, c, m))
    for q in range(pieces):
        own = a_ref.at[pl.ds(q * size, size)]
        send(own, piece(l, c, q), up_sem.at[l, c, q], a_recv.at[l, c, q], (i, c + 1, l), c + 1 < n_col)
        send(own, piece(l, c, q), down_sem.at[l, c, q], a_recv.at[l, c, q], (i, c - 1, l), c >= 1)
        send(own, piece(l, c, q), over_sem.at[l, c, q], a_recv.at[l, c, q], (i, c, m))
    for dr in range(1, n_row):
        to = (lax.rem(i + dr, n_row), c, l)
        send(b_ref, b_all.at[l, i], b_send.at[dr], b_recv.at[l, i], to)
    mine = [
        pltpu.make_async_copy(a_ref, a_all.at[l, c], own_sem.at[0]),
        pltpu.make_async_copy(am_ref, am_all.at[l, c], own_sem.at[1]),
        pltpu.make_async_copy(b_ref, b_all.at[l, i], own_sem.at[2]),
        pltpu.make_async_copy(bm_ref, bm_all.at[l, i], own_sem.at[3]),
    ]
    for copy in mine:
        copy.start()

    arrived(b_all.at[m, i], b_recv.at[m, i])
    for dr in range(1, n_row):
        to = (lax.rem(i + dr, n_row), c, l)
        send(b_all.at[m, i], b_all.at[m, i], b_pass.at[dr], b_recv.at[m, i], to)

    for d in range(1, n_col):
        for q in range(pieces):
            low, high = c - d, c + d
            over_low = low >= 0
            over_high = high < n_col
            if d == 1 and short_cuts:
                over_low = (c >= 2) & (c < n_col - 1) if q < half else c >= 2
                over_high = (c >= 1) & (c < n_col - 2) if q < half else c < n_col - 2

            @pl.when(low >= 0)
            def _():
                arrived(piece(l, low, q), a_recv.at[l, low, q])

            part = piece(l, low, q)
            send(part, part, up_sem.at[l, low, q], a_recv.at[l, low, q], (i, c + 1, l),
                 (low >= 0) & (c + 1 < n_col))
            send(part, part, over_sem.at[l, low, q], a_recv.at[l, low, q], (i, c, m), over_low)

            @pl.when(high < n_col)
            def _():
                arrived(piece(l, high, q), a_recv.at[l, high, q])

            part = piece(l, high, q)
            send(part, part, down_sem.at[l, high, q], a_recv.at[l, high, q], (i, c - 1, l),
                 (high < n_col) & (c >= 1))
            send(part, part, over_sem.at[l, high, q], a_recv.at[l, high, q], (i, c, m), over_high)

            if d == 1:
                part = piece(m, c, q)
                arrived(part, a_recv.at[m, c, q])
                if short_cuts:
                    up = c == 0
                    down = c == n_col - 1
                    if q < half:
                        up = up | (c == n_col - 2)
                        down = down | (c == 1)
                    send(part, part, up_sem.at[m, c, q], a_recv.at[m, c, q], (i, c + 1, l), up)
                    send(part, part, down_sem.at[m, c, q], a_recv.at[m, c, q], (i, c - 1, l), down)

    for d in range(1, n_col):
        other = lax.rem(c + d, n_col)
        for q in range(pieces):
            arrived(piece(m, other, q), a_recv.at[m, other, q])
    for ll, cc in [(lax.rem(l + k // n_col, n_layer), lax.rem(c + k % n_col, n_col))
                   for k in range(1, n_layer * n_col)]:
        arrived(am_all.at[ll, cc], am_recv.at[ll, cc])
    for k in range(1, n_layer * n_row):
        ll, rr = lax.rem(l + k // n_row, n_layer), lax.rem(i + k % n_row, n_row)
        arrived(bm_all.at[ll, rr], bm_recv.at[ll, rr])
        if k != n_row:
            arrived(b_all.at[ll, rr], b_recv.at[ll, rr])
    for copy in mine:
        copy.wait()
    for copy, when in sent:
        if when is None:
            copy().wait_send()
        else:
            pl.when(when)(lambda copy=copy: copy().wait_send())


def gather(a, am, b, bm, n_row, n_col, n_layer):
    pieces = 4 if a.shape[0] % 4 == 0 else 1
    any_space = pl.BlockSpec(memory_space=pl.ANY)
    dma = pltpu.SemaphoreType.DMA
    return pl.pallas_call(
        functools.partial(gather_kernel, n_row, n_col, n_layer, pieces),
        out_shape=(
            jax.ShapeDtypeStruct((n_layer, n_col) + a.shape, a.dtype),
            jax.ShapeDtypeStruct((n_layer, n_col) + am.shape, am.dtype),
            jax.ShapeDtypeStruct((n_layer, n_row) + b.shape, b.dtype),
            jax.ShapeDtypeStruct((n_layer, n_row) + bm.shape, bm.dtype),
        ),
        in_specs=[any_space] * 4,
        out_specs=(any_space,) * 4,
        scratch_shapes=[
            dma((n_layer, n_col, pieces)),
            dma((n_layer, n_col, pieces)),
            dma((n_layer, n_col, pieces)),
            dma((n_layer, n_col, pieces)),
            dma((n_layer * n_col,)),
            dma((n_layer, n_col)),
            dma((n_row,)),
            dma((n_row,)),
            dma((n_layer, n_row)),
            dma((n_layer * n_row,)),
            dma((n_layer, n_row)),
            dma((4,)),
        ],
        compiler_params=pltpu.CompilerParams(collective_id=0, has_side_effects=True),
    )(a, am, b, bm)


def product_kernel(n_row, n_col, where, am, bm, a_ref, b_ref, out_ref, left, right):
    layer, turn = pl.program_id(0), pl.program_id(1)
    i, j, l = where[0], where[1], where[2]
    block = a_ref.shape[-1]
    width = out_ref.shape[1] // block
    group = lax.rem(i + turn, n_col)
    stack = group // n_row
    source = lax.rem(lax.rem(group, n_row) - lax.rem(j, n_row) + n_row, n_row)

    @pl.when((layer == 0) & (turn == 0))
    def _():
        out_ref[...] = jnp.zeros_like(out_ref)

    left[...] = jnp.zeros_like(left)
    right[...] = jnp.zeros_like(right)
    for s in range(a_ref.shape[2]):
        p = am[layer, turn, 0, s]

        @pl.when(p >= 0)
        def _():
            r = pl.multiple_of(p // KB * block, block)
            k = pl.multiple_of(lax.rem(p, KB) * block, block)
            left[pl.ds(r, block), pl.ds(k, block)] = a_ref[0, 0, s]

    for s in range(b_ref.shape[3]):
        p = bm[layer, source, 0, stack * b_ref.shape[3] + s]
        col = lax.rem(p, CB) - l * width

        @pl.when((p >= 0) & (col >= 0) & (col < width))
        def _():
            r = pl.multiple_of(p // CB * block, block)
            k = pl.multiple_of(col * block, block)
            right[pl.ds(r, block), pl.ds(k, block)] = b_ref[layer, source, stack, s]

    out_ref[...] += jnp.dot(left[...], right[...], preferred_element_type=jnp.float32)


def product(where, a_all, am, b_all, bm, n_row, n_col, n_layer):
    block = a_all.shape[-1]
    width = CB * block // n_layer
    return pl.pallas_call(
        functools.partial(product_kernel, n_row, n_col),
        out_shape=jax.ShapeDtypeStruct((RB * block, width), jnp.float32),
        grid_spec=pltpu.PrefetchScalarGridSpec(
            num_scalar_prefetch=3,
            grid=(n_layer, n_col),
            in_specs=[
                pl.BlockSpec((1, 1) + a_all.shape[2:], lambda g, t, *_: (g, t, 0, 0, 0)),
                pl.BlockSpec(memory_space=pltpu.VMEM),
            ],
            out_specs=pl.BlockSpec((RB * block, width), lambda g, t, *_: (0, 0)),
            scratch_shapes=[
                pltpu.VMEM((RB * block, KB * block), jnp.bfloat16),
                pltpu.VMEM((KB * block, width), jnp.bfloat16),
            ],
        ),
        compiler_params=pltpu.CompilerParams(vmem_limit_bytes=40 * 1024 * 1024),
    )(where, am, bm, a_all, b_all)


def masked(pos, count):
    slots = jnp.arange(pos.shape[-1], dtype=jnp.int32)
    flat = jnp.where(slots < count[..., None], pos, -1).reshape(1, -1)
    return jnp.pad(flat, ((0, 0), (0, 128 - flat.shape[1])), constant_values=-1)


def per_device(a_vals, a_pos, a_count, b_vals, b_pos, b_count):
    n_row = lax.axis_size("row")
    n_col = lax.axis_size("col")
    n_layer = lax.axis_size("layer")
    where = jnp.stack([lax.axis_index(name) for name in ("row", "col", "layer")]).astype(jnp.int32)
    am = masked(a_pos[0, 0, 0], a_count[0, 0, 0])
    bm = masked(b_pos[0, 0, 0], b_count[0, 0, 0])
    a_all, am_all, b_all, bm_all = gather(
        a_vals[0, 0, 0], am, b_vals[0, 0, 0], bm, n_row, n_col, n_layer)
    return product(where, a_all, am_all, b_all, bm_all, n_row, n_col, n_layer)


def solution(mesh):
    placed = (
        P("row", "col", "layer", None, None, None),
        P("row", "col", "layer", None),
        P("row", "col", "layer"),
        P("row", "col", "layer", None, None, None, None),
        P("row", "col", "layer", None, None),
        P("row", "col", "layer", None),
    )
    return jax.shard_map(
        per_device,
        mesh=mesh,
        in_specs=placed,
        out_specs=P("row", ("col", "layer")),
        check_vma=False,
    )
```

```python
import functools

import jax
import jax.numpy as jnp
from jax import lax
from jax.experimental import pallas as pl
from jax.experimental.pallas import tpu as pltpu
from jax.sharding import PartitionSpec as P

KB = 4
CB = 8
RB = 8
MESH = pl.DeviceIdType.MESH


def kernel(n_row, n_col, n_layer, pieces, a_ref, b_ref, map_ref, out_ref, *scratch):
    scratch = list(scratch)
    a_all = [[scratch.pop(0) for _ in range(n_col)] for _ in range(n_layer)]
    b_all = [[scratch.pop(0) for _ in range(n_row)] for _ in range(n_layer)]
    (a_maps, b_maps, a_places, b_places, left, right,
     up_sem, down_sem, over_sem, a_recv, am_send, am_recv,
     b_send, b_pass, b_recv, bm_send, bm_recv, own_sem) = scratch
    i = lax.axis_index("row")
    c = lax.axis_index("col")
    l = lax.axis_index("layer")
    m = 1 - l
    slots = a_ref.shape[0]
    slots_b = b_ref.shape[0]
    block = a_ref.shape[-1]
    width = out_ref.shape[1] // block
    size = slots // pieces
    half = pieces // 2
    short_cuts = n_col >= 4

    peers = [(dl, dc) for dl in range(n_layer) for dc in range(n_col) if dl or dc]
    sides = [(dl, dr) for dl in range(n_layer) for dr in range(n_row) if dl or dr]

    def peer(dl, dc):
        return (i, lax.rem(c + dc, n_col), lax.rem(l + dl, n_layer))

    def side(dl, dr):
        return (lax.rem(i + dr, n_row), c, lax.rem(l + dl, n_layer))

    barrier = pltpu.get_barrier_semaphore()
    greeted = [peer(*one) for one in peers] + [side(*one) for one in sides if one[1]]
    for one in greeted:
        pl.semaphore_signal(barrier, inc=1, device_id=one, device_id_type=MESH)
    mine = [
        pltpu.make_async_copy(a_ref, a_all[0][0].at[pl.ds(0, slots)], own_sem.at[0]),
        pltpu.make_async_copy(b_ref, b_all[0][0].at[pl.ds(0, slots_b)], own_sem.at[1]),
        pltpu.make_async_copy(map_ref, a_maps.at[0, 0], own_sem.at[2]),
        pltpu.make_async_copy(map_ref, b_maps.at[0, 0], own_sem.at[3]),
    ]
    for copy in mine:
        copy.start()
    for ref in [one for layer in a_all for one in layer]:
        ref[slots] = jnp.zeros((block, block), ref.dtype)
    for ref in [one for layer in b_all for one in layer]:
        ref[slots_b] = jnp.zeros((block, block), ref.dtype)
    pl.semaphore_wait(barrier, len(greeted))

    sent = []

    def send(src, dst, s_sem, r_sem, to, when=None):
        def copy():
            return pltpu.make_async_remote_copy(
                src_ref=src, dst_ref=dst, send_sem=s_sem, recv_sem=r_sem,
                device_id=to, device_id_type=MESH)

        if when is None:
            copy().start()
        else:
            pl.when(when)(lambda: copy().start())
        sent.append((copy, when))

    def arrived(dst, r_sem):
        pltpu.make_async_copy(dst, dst, r_sem).wait()

    def piece(dl, dc, q):
        return a_all[dl][dc].at[pl.ds(q * size, size)]

    def stored(dl, dr):
        return b_all[dl][dr].at[pl.ds(0, slots_b)]

    def back(dl, dc, n):
        return (n_layer - dl) % n_layer, (n - dc) % n

    for k, one in enumerate(peers):
        dl, dc = back(*one, n_col)
        send(map_ref, a_maps.at[dl, dc], am_send.at[k], am_recv.at[dl, dc], peer(*one))
    for k, one in enumerate(sides):
        dl, dr = back(*one, n_row)
        send(map_ref, b_maps.at[dl, dr], bm_send.at[k], bm_recv.at[dl, dr], side(*one))

    below, above, across = (i, c - 1, l), (i, c + 1, l), (i, c, m)
    send(b_ref, stored(1, 0), b_send.at[0], b_recv.at[1, 0], across)
    for q in range(pieces):
        own = a_ref.at[pl.ds(q * size, size)]
        send(own, piece(0, n_col - 1, q), up_sem.at[0, 0, q], a_recv.at[0, n_col - 1, q], above, c + 1 < n_col)
        send(own, piece(0, 1, q), down_sem.at[0, 0, q], a_recv.at[0, 1, q], below, c >= 1)
        send(own, piece(1, 0, q), over_sem.at[0, 0, q], a_recv.at[1, 0, q], across)
    for dr in range(1, n_row):
        send(b_ref, stored(0, n_row - dr), b_send.at[dr], b_recv.at[0, n_row - dr], side(0, dr))

    arrived(stored(1, 0), b_recv.at[1, 0])
    for dr in range(1, n_row):
        send(stored(1, 0), stored(1, n_row - dr), b_pass.at[dr], b_recv.at[1, n_row - dr], side(0, dr))

    for dl, dc in peers:
        arrived(a_maps.at[dl, dc], am_recv.at[dl, dc])
    for dl, dr in sides:
        arrived(b_maps.at[dl, dr], bm_recv.at[dl, dr])
    for copy in mine:
        copy.wait()
    tables = [
        pltpu.make_async_copy(a_maps, a_places, own_sem.at[4]),
        pltpu.make_async_copy(b_maps, b_places, own_sem.at[5]),
    ]
    for copy in tables:
        copy.start()
    for copy in tables:
        copy.wait()

    def multiply(dl, dc, first=False):
        dr = dc % n_row
        a, b = a_all[dl][dc], b_all[dl][dr]
        stack = lax.div(lax.rem(i + c + dc, n_col), n_row)
        base = RB * KB + stack * KB * CB + l * width
        for k in range(KB):
            for n in range(width):
                slot = b_places[dl, dr, 0, base + k * CB + n]
                right[k * block:(k + 1) * block, n * block:(n + 1) * block] = b[slot]
        for r in range(RB):
            for k in range(KB):
                slot = a_places[dl, dc, 0, r * KB + k]
                left[r * block:(r + 1) * block, k * block:(k + 1) * block] = a[slot]
        term = jnp.dot(left[...], right[...], preferred_element_type=jnp.float32)
        if first:
            out_ref[...] = term
        else:
            out_ref[...] += term

    def at_distance(d, dl):
        def low():
            multiply(dl, n_col - d)

        def high():
            multiply(dl, d)

        def low_wait():
            for q in range(pieces):
                arrived(piece(dl, n_col - d, q), a_recv.at[dl, n_col - d, q])

        def high_wait():
            for q in range(pieces):
                arrived(piece(dl, d, q), a_recv.at[dl, d, q])

        def one(condition, wait, body):
            def run():
                @pl.when(condition)
                def _():
                    if dl:
                        wait()
                    body()
            return run

        return [one(c >= d, low_wait, low), one(c + d < n_col, high_wait, high)]

    def gram():
        for dl, dr in sides:
            if (dl, dr) != (1, 0):
                arrived(stored(dl, dr), b_recv.at[dl, dr])

    todo = [lambda: multiply(0, 0, True)]
    for d in range(1, n_col):
        for q in range(pieces):
            low, high = n_col - d, d
            over_low = c >= d
            over_high = c + d < n_col
            if d == 1 and short_cuts:
                over_low = (c >= 2) & (c < n_col - 1) if q < half else c >= 2
                over_high = (c >= 1) & (c < n_col - 2) if q < half else c < n_col - 2

            @pl.when(c >= d)
            def _():
                arrived(piece(0, low, q), a_recv.at[0, low, q])

            part = piece(0, low, q)
            if low > 1:
                send(part, piece(0, low - 1, q), up_sem.at[0, low, q], a_recv.at[0, low - 1, q], above,
                     (c >= d) & (c + 1 < n_col))
            send(part, piece(1, low, q), over_sem.at[0, low, q], a_recv.at[1, low, q], across, over_low)

            @pl.when(c + d < n_col)
            def _():
                arrived(piece(0, high, q), a_recv.at[0, high, q])

            part = piece(0, high, q)
            if high + 1 < n_col:
                send(part, piece(0, high + 1, q), down_sem.at[0, high, q], a_recv.at[0, high + 1, q], below,
                     (c + d < n_col) & (c >= 1))
            send(part, piece(1, high, q), over_sem.at[1, high, q], a_recv.at[1, high, q], across, over_high)

            if d == 1:
                part = piece(1, 0, q)
                arrived(part, a_recv.at[1, 0, q])
                if short_cuts:
                    up = c == 0
                    down = c == n_col - 1
                    if q < half:
                        up = up | (c == n_col - 2)
                        down = down | (c == 1)
                    send(part, piece(1, n_col - 1, q), up_sem.at[1, 0, q], a_recv.at[1, n_col - 1, q], above, up)
                    send(part, piece(1, 1, q), down_sem.at[1, 0, q], a_recv.at[1, 1, q], below, down)
            if todo:
                todo.pop(0)()
        while todo:
            todo.pop(0)()
        todo = at_distance(d, 0)
        if d == 1:
            todo = [gram] + todo + [lambda: multiply(1, 0)]
        else:
            todo = todo + at_distance(d - 1, 1)
    todo = todo + at_distance(n_col - 1, 1)
    for one in todo:
        one()
    for copy, when in sent:
        if when is None:
            copy().wait_send()
        else:
            pl.when(when)(lambda copy=copy: copy().wait_send())


def place_map(pos, count, places):
    slots = pos.shape[-1]
    order = jnp.arange(slots, dtype=jnp.int32)
    free = jnp.where(order < count, pos, -1)
    hit = free[:, None] == jnp.arange(places, dtype=jnp.int32)[None, :]
    return jnp.min(jnp.where(hit, order[:, None], slots), axis=0)


def per_device(a_vals, a_pos, a_count, b_vals, b_pos, b_count):
    n_row = lax.axis_size("row")
    n_col = lax.axis_size("col")
    n_layer = lax.axis_size("layer")
    a = a_vals[0, 0, 0]
    stacks, slots_b = b_pos.shape[-2:]
    block = a.shape[-1]
    b = b_vals[0, 0, 0].reshape(stacks * slots_b, block, block)
    rows = [place_map(a_pos[0, 0, 0], a_count[0, 0, 0], RB * KB)]
    for h in range(stacks):
        one = place_map(b_pos[0, 0, 0, h], b_count[0, 0, 0, h], KB * CB)
        rows.append(jnp.where(one == slots_b, stacks * slots_b, one + h * slots_b))
    places = jnp.concatenate(rows)
    places = jnp.pad(places, (0, 128 - places.shape[0]))[None]
    pieces = 4 if a.shape[0] % 4 == 0 else 1
    width = CB * block // n_layer
    dma = pltpu.SemaphoreType.DMA
    any_space = pl.BlockSpec(memory_space=pl.ANY)
    maps = ((n_layer, n_col, 1, 128), (n_layer, n_row, 1, 128))
    return pl.pallas_call(
        functools.partial(kernel, n_row, n_col, n_layer, pieces),
        out_shape=jax.ShapeDtypeStruct((RB * block, width), jnp.float32),
        in_specs=[any_space] * 3,
        out_specs=pl.BlockSpec(memory_space=pltpu.VMEM),
        scratch_shapes=[pltpu.VMEM((a.shape[0] + 1, block, block), a.dtype)] * (n_layer * n_col)
        + [pltpu.VMEM((b.shape[0] + 1, block, block), b.dtype)] * (n_layer * n_row)
        + [
            pltpu.VMEM(maps[0], jnp.int32),
            pltpu.VMEM(maps[1], jnp.int32),
            pltpu.SMEM(maps[0], jnp.int32),
            pltpu.SMEM(maps[1], jnp.int32),
            pltpu.VMEM((RB * block, KB * block), a.dtype),
            pltpu.VMEM((KB * block, width), b.dtype),
            dma((n_layer, n_col, pieces)),
            dma((n_layer, n_col, pieces)),
            dma((n_layer, n_col, pieces)),
            dma((n_layer, n_col, pieces)),
            dma((n_layer * n_col,)),
            dma((n_layer, n_col)),
            dma((n_row,)),
            dma((n_row,)),
            dma((n_layer, n_row)),
            dma((n_layer * n_row,)),
            dma((n_layer, n_row)),
            dma((6,)),
        ],
        compiler_params=pltpu.CompilerParams(
            collective_id=0, has_side_effects=True, vmem_limit_bytes=52 * 1024 * 1024),
    )(a, b, places)


def solution(mesh):
    placed = (
        P("row", "col", "layer", None, None, None),
        P("row", "col", "layer", None),
        P("row", "col", "layer"),
        P("row", "col", "layer", None, None, None, None),
        P("row", "col", "layer", None, None),
        P("row", "col", "layer", None),
    )
    return jax.shard_map(
        per_device,
        mesh=mesh,
        in_specs=placed,
        out_specs=P("row", ("col", "layer")),
        check_vma=False,
    )
```

```python
import functools

import jax
import jax.numpy as jnp
from jax import lax
from jax.experimental import pallas as pl
from jax.experimental.pallas import tpu as pltpu
from jax.sharding import PartitionSpec as P

KB = 4
CB = 8
RB = 8
MESH = pl.DeviceIdType.MESH


def kernel(n_row, n_col, n_layer, pieces,
           a_ref, b_ref, a_pos, a_count, b_pos, b_count, out_ref, *scratch):
    scratch = list(scratch)
    a_all = [[scratch.pop(0) for _ in range(n_col)] for _ in range(n_layer)]
    b_all = [[scratch.pop(0) for _ in range(n_row)] for _ in range(n_layer)]
    (a_maps, b_maps, a_places, b_places, a_pos_s, a_count_s, b_pos_s, b_count_s, left, right,
     up_sem, down_sem, over_sem, a_recv, am_send, am_recv,
     b_send, b_pass, b_recv, bm_send, bm_recv, own_sem, late_sem) = scratch
    i = lax.axis_index("row")
    c = lax.axis_index("col")
    l = lax.axis_index("layer")
    m = 1 - l
    slots = a_ref.shape[0]
    slots_b = b_ref.shape[0]
    block = a_ref.shape[-1]
    width = out_ref.shape[1] // block
    size = slots // pieces
    half = (pieces * 5 + 4) // 8
    short_cuts = n_col >= 4

    peers = [(dl, dc) for dl in range(n_layer) for dc in range(n_col) if dl or dc]
    sides = [(dl, dr) for dl in range(n_layer) for dr in range(n_row) if dl or dr]

    def peer(dl, dc):
        return (i, lax.rem(c + dc, n_col), lax.rem(l + dl, n_layer))

    def side(dl, dr):
        return (lax.rem(i + dr, n_row), c, lax.rem(l + dl, n_layer))

    barrier = pltpu.get_barrier_semaphore()
    greeted = [peer(*one) for one in peers] + [side(*one) for one in sides if one[1]]
    for one in greeted:
        pl.semaphore_signal(barrier, inc=1, device_id=one, device_id_type=MESH)
    mine = [
        pltpu.make_async_copy(a_ref, a_all[0][0].at[pl.ds(0, slots)], own_sem.at[0]),
        pltpu.make_async_copy(b_ref, b_all[0][0].at[pl.ds(0, slots_b)], own_sem.at[1]),
    ]
    small = [
        pltpu.make_async_copy(a_pos, a_pos_s, own_sem.at[2]),
        pltpu.make_async_copy(a_count, a_count_s, own_sem.at[3]),
        pltpu.make_async_copy(b_pos, b_pos_s, own_sem.at[6]),
        pltpu.make_async_copy(b_count, b_count_s, own_sem.at[7]),
    ]
    for copy in small + mine:
        copy.start()
    for ref in [one for layer in a_all for one in layer]:
        ref[slots] = jnp.zeros((block, block), ref.dtype)
    for ref in [one for layer in b_all for one in layer]:
        ref[slots_b] = jnp.zeros((block, block), ref.dtype)
    for copy in small:
        copy.wait()
    lane = lax.broadcasted_iota(jnp.int32, (1, 128), 1)
    places = jnp.where(lane < RB * KB, slots, slots_b)
    for s in range(slots):
        places = jnp.where((lane == a_pos_s[0, s]) & (s < a_count_s[0, 0]), s, places)
    for h in range(b_pos_s.shape[0]):
        start = RB * KB + h * KB * CB
        for s in range(b_pos_s.shape[1]):
            hit = (lane == start + b_pos_s[h, s]) & (s < b_count_s[0, h])
            places = jnp.where(hit, h * b_pos_s.shape[1] + s, places)
    a_maps[0, 0] = places
    b_maps[0, 0] = places
    map_ref = a_maps.at[0, 0]
    pl.semaphore_wait(barrier, len(greeted))

    sent = []

    def send(src, dst, s_sem, r_sem, to, when=None):
        def copy():
            return pltpu.make_async_remote_copy(
                src_ref=src, dst_ref=dst, send_sem=s_sem, recv_sem=r_sem,
                device_id=to, device_id_type=MESH)

        if when is None:
            copy().start()
        else:
            pl.when(when)(lambda: copy().start())
        sent.append((copy, when))

    def arrived(dst, r_sem):
        pltpu.make_async_copy(dst, dst, r_sem).wait()

    def piece(dl, dc, q):
        return a_all[dl][dc].at[pl.ds(q * size, size)]

    def stored(dl, dr):
        return b_all[dl][dr].at[pl.ds(0, slots_b)]

    def back(dl, dc, n):
        return (n_layer - dl) % n_layer, (n - dc) % n

    for k, one in enumerate(peers):
        dl, dc = back(*one, n_col)
        send(map_ref, a_maps.at[dl, dc], am_send.at[k], am_recv.at[dl, dc], peer(*one))
    for k, one in enumerate(sides):
        dl, dr = back(*one, n_row)
        send(map_ref, b_maps.at[dl, dr], bm_send.at[k], bm_recv.at[dl, dr], side(*one))

    below, above, across = (i, c - 1, l), (i, c + 1, l), (i, c, m)
    send(b_ref, stored(1, 0), b_send.at[0], b_recv.at[1, 0], across)
    for q in range(pieces):
        own = a_ref.at[pl.ds(q * size, size)]
        send(own, piece(0, n_col - 1, q), up_sem.at[0, 0, q], a_recv.at[0, n_col - 1, q], above, c + 1 < n_col)
        send(own, piece(0, 1, q), down_sem.at[0, 0, q], a_recv.at[0, 1, q], below, c >= 1)
        send(own, piece(1, 0, q), over_sem.at[0, 0, q], a_recv.at[1, 0, q], across)
    for dr in range(1, n_row):
        send(b_ref, stored(0, n_row - dr), b_send.at[dr], b_recv.at[0, n_row - dr], side(0, dr))

    arrived(stored(1, 0), b_recv.at[1, 0])
    for dr in range(1, n_row):
        send(stored(1, 0), stored(1, n_row - dr), b_pass.at[dr], b_recv.at[1, n_row - dr], side(0, dr))

    for dl, dc in peers:
        arrived(a_maps.at[dl, dc], am_recv.at[dl, dc])
    for dl, dr in sides:
        arrived(b_maps.at[dl, dr], bm_recv.at[dl, dr])
    for copy in mine:
        copy.wait()
    tables = [
        pltpu.make_async_copy(a_maps, a_places, own_sem.at[4]),
        pltpu.make_async_copy(b_maps, b_places, own_sem.at[5]),
    ]
    for copy in tables:
        copy.start()
    for copy in tables:
        copy.wait()

    def multiply(dl, dc, first=False):
        dr = dc % n_row
        a, b = a_all[dl][dc], b_all[dl][dr]
        stack = lax.div(lax.rem(i + c + dc, n_col), n_row)
        base = RB * KB + stack * KB * CB + l * width
        for k in range(KB):
            for n in range(width):
                slot = b_places[dl, dr, 0, base + k * CB + n]
                right[k * block:(k + 1) * block, n * block:(n + 1) * block] = b[slot]
        for r in range(RB):
            for k in range(KB):
                slot = a_places[dl, dc, 0, r * KB + k]
                left[r * block:(r + 1) * block, k * block:(k + 1) * block] = a[slot]
        term = jnp.dot(left[...], right[...], preferred_element_type=jnp.float32)
        if first:
            out_ref[...] = term
        else:
            out_ref[...] += term

    def at_distance(d, dl):
        def low():
            multiply(dl, n_col - d)

        def high():
            multiply(dl, d)

        def low_wait():
            for q in range(pieces):
                arrived(piece(dl, n_col - d, q), a_recv.at[dl, n_col - d, q])

        def high_wait():
            for q in range(pieces):
                arrived(piece(dl, d, q), a_recv.at[dl, d, q])

        def one(condition, wait, body):
            def run():
                @pl.when(condition)
                def _():
                    if dl:
                        wait()
                    body()
            return run

        return [one(c >= d, low_wait, low), one(c + d < n_col, high_wait, high)]

    def gram():
        for dl, dr in sides:
            if (dl, dr) != (1, 0):
                arrived(stored(dl, dr), b_recv.at[dl, dr])

    todo = [lambda: multiply(0, 0, True)]
    for d in range(1, n_col):
        for q in range(pieces):
            low, high = n_col - d, d
            over_low = c >= d
            over_high = c + d < n_col
            if d == 1 and short_cuts:
                over_low = (c >= 2) & (c < n_col - 1) if q < half else c >= 2
                over_high = (c >= 1) & (c < n_col - 2) if q < half else c < n_col - 2

            @pl.when(c >= d)
            def _():
                arrived(piece(0, low, q), a_recv.at[0, low, q])

            part = piece(0, low, q)
            if low > 1:
                send(part, piece(0, low - 1, q), up_sem.at[0, low, q], a_recv.at[0, low - 1, q], above,
                     (c >= d) & (c + 1 < n_col))
            send(part, piece(1, low, q), over_sem.at[0, low, q], a_recv.at[1, low, q], across, over_low)

            @pl.when(c + d < n_col)
            def _():
                arrived(piece(0, high, q), a_recv.at[0, high, q])

            part = piece(0, high, q)
            if high + 1 < n_col:
                send(part, piece(0, high + 1, q), down_sem.at[0, high, q], a_recv.at[0, high + 1, q], below,
                     (c + d < n_col) & (c >= 1))
            send(part, piece(1, high, q), over_sem.at[1, high, q], a_recv.at[1, high, q], across, over_high)

            if d == 1:
                part = piece(1, 0, q)
                arrived(part, a_recv.at[1, 0, q])
                if short_cuts:
                    up = c == 0
                    down = c == n_col - 1
                    send(part, piece(1, n_col - 1, q), up_sem.at[1, 0, q], a_recv.at[1, n_col - 1, q], above, up)
                    send(part, piece(1, 1, q), down_sem.at[1, 0, q], a_recv.at[1, 1, q], below, down)
            if todo:
                todo.pop(0)()
        if d == n_col - 2 and short_cuts:
            for q in range(half):
                part = piece(1, 0, q)
                send(part, piece(1, n_col - 1, q), late_sem.at[0, q], a_recv.at[1, n_col - 1, q], above, c == n_col - 2)
                send(part, piece(1, 1, q), late_sem.at[1, q], a_recv.at[1, 1, q], below, c == 1)
        while todo:
            todo.pop(0)()
        todo = at_distance(d, 0)
        if d == 1:
            todo = [gram] + todo + [lambda: multiply(1, 0)]
        else:
            todo = todo + at_distance(d - 1, 1)
    todo = todo + at_distance(n_col - 1, 1)
    for one in todo:
        one()
    for copy, when in sent:
        if when is None:
            copy().wait_send()
        else:
            pl.when(when)(lambda copy=copy: copy().wait_send())


def write_kernel(in_ref, out_ref):
    out_ref[...] = in_ref[...]


def write(total):
    one = pl.BlockSpec((total.shape[0] // 4, total.shape[1]), lambda n: (n, 0))
    return pl.pallas_call(
        write_kernel,
        out_shape=jax.ShapeDtypeStruct(total.shape, total.dtype),
        grid=(4,),
        in_specs=[one],
        out_specs=one,
        compiler_params=pltpu.CompilerParams(vmem_limit_bytes=63 * 1024 * 1024),
    )(total)


def per_device(a_vals, a_pos, a_count, b_vals, b_pos, b_count):
    n_row = lax.axis_size("row")
    n_col = lax.axis_size("col")
    n_layer = lax.axis_size("layer")
    a = a_vals[0, 0, 0]
    stacks, slots_b = b_pos.shape[-2:]
    block = a.shape[-1]
    b = b_vals[0, 0, 0].reshape(stacks * slots_b, block, block)
    pieces = max(1, 32 // n_col)
    if a.shape[0] % pieces:
        pieces = 1
    width = CB * block // n_layer
    dma = pltpu.SemaphoreType.DMA
    in_hbm = pl.BlockSpec(memory_space=pltpu.HBM)
    maps = ((n_layer, n_col, 1, 128), (n_layer, n_row, 1, 128))
    total = pl.pallas_call(
        functools.partial(kernel, n_row, n_col, n_layer, pieces),
        out_shape=jax.ShapeDtypeStruct((RB * block, width), jnp.float32),
        in_specs=[in_hbm] * 6,
        out_specs=pl.BlockSpec(memory_space=pltpu.VMEM),
        scratch_shapes=[pltpu.VMEM((a.shape[0] + 1, block, block), a.dtype)] * (n_layer * n_col)
        + [pltpu.VMEM((b.shape[0] + 1, block, block), b.dtype)] * (n_layer * n_row)
        + [
            pltpu.VMEM(maps[0], jnp.int32),
            pltpu.VMEM(maps[1], jnp.int32),
            pltpu.SMEM(maps[0], jnp.int32),
            pltpu.SMEM(maps[1], jnp.int32),
            pltpu.SMEM((1, a_pos.shape[-1]), jnp.int32),
            pltpu.SMEM((1, 1), jnp.int32),
            pltpu.SMEM((stacks, slots_b), jnp.int32),
            pltpu.SMEM((1, stacks), jnp.int32),
            pltpu.VMEM((RB * block, KB * block), a.dtype),
            pltpu.VMEM((KB * block, width), b.dtype),
            dma((n_layer, n_col, pieces)),
            dma((n_layer, n_col, pieces)),
            dma((n_layer, n_col, pieces)),
            dma((n_layer, n_col, pieces)),
            dma((n_layer * n_col,)),
            dma((n_layer, n_col)),
            dma((n_row,)),
            dma((n_row,)),
            dma((n_layer, n_row)),
            dma((n_layer * n_row,)),
            dma((n_layer, n_row)),
            dma((8,)),
            dma((2, pieces)),
        ],
        compiler_params=pltpu.CompilerParams(
            collective_id=0, has_side_effects=True, vmem_limit_bytes=63 * 1024 * 1024),
    )(a, b, a_pos[0, 0], a_count[0], b_pos[0, 0, 0], b_count[0, 0])
    return write(total)


def solution(mesh):
    placed = (
        P("row", "col", "layer", None, None, None),
        P("row", "col", "layer", None),
        P("row", "col", "layer"),
        P("row", "col", "layer", None, None, None, None),
        P("row", "col", "layer", None, None),
        P("row", "col", "layer", None),
    )
    return jax.shard_map(
        per_device,
        mesh=mesh,
        in_specs=placed,
        out_specs=P("row", ("col", "layer")),
        check_vma=False,
    )
```

```python
import functools

import jax
import jax.numpy as jnp
from jax import lax
from jax.experimental import pallas as pl
from jax.experimental.pallas import tpu as pltpu
from jax.sharding import PartitionSpec as P

KB = 4
CB = 8
RB = 8
IN_FLIGHT = 2
MESH = pl.DeviceIdType.MESH


def kernel(n_row, n_col, n_layer, pieces,
           a_ref, b_ref, a_pos, a_count, b_pos, b_count, out_ref, *scratch):
    scratch = list(scratch)
    a_all = [[scratch.pop(0) for _ in range(n_col)] for _ in range(n_layer)]
    b_all = [[scratch.pop(0) for _ in range(n_row)] for _ in range(n_layer)]
    (a_maps, b_maps, a_places, b_places, a_pos_s, a_count_s, b_pos_s, b_count_s, left, right,
     up_sem, down_sem, over_sem, a_recv, am_send, am_recv,
     b_send, b_pass, b_recv, bm_send, bm_recv, own_sem, late_sem) = scratch
    i = lax.axis_index("row")
    c = lax.axis_index("col")
    l = lax.axis_index("layer")
    m = 1 - l
    slots = a_ref.shape[0]
    slots_b = b_ref.shape[0]
    block = a_ref.shape[-1]
    width = out_ref.shape[1] // block
    size = slots // pieces
    half = (pieces * 5 + 4) // 8
    short_cuts = n_col >= 4

    peers = [(dl, dc) for dl in range(n_layer) for dc in range(n_col) if dl or dc]
    sides = [(dl, dr) for dl in range(n_layer) for dr in range(n_row) if dl or dr]

    def peer(dl, dc):
        return (i, lax.rem(c + dc, n_col), lax.rem(l + dl, n_layer))

    def side(dl, dr):
        return (lax.rem(i + dr, n_row), c, lax.rem(l + dl, n_layer))

    barrier = pltpu.get_barrier_semaphore()
    greeted = [peer(*one) for one in peers] + [side(*one) for one in sides if one[1]]
    for one in greeted:
        pl.semaphore_signal(barrier, inc=1, device_id=one, device_id_type=MESH)
    mine = [
        pltpu.make_async_copy(a_ref, a_all[0][0].at[pl.ds(0, slots)], own_sem.at[0]),
        pltpu.make_async_copy(b_ref, b_all[0][0].at[pl.ds(0, slots_b)], own_sem.at[1]),
    ]
    small = [
        pltpu.make_async_copy(a_pos, a_pos_s, own_sem.at[2]),
        pltpu.make_async_copy(a_count, a_count_s, own_sem.at[3]),
        pltpu.make_async_copy(b_pos, b_pos_s, own_sem.at[6]),
        pltpu.make_async_copy(b_count, b_count_s, own_sem.at[7]),
    ]
    for copy in small + mine:
        copy.start()
    for ref in [one for layer in a_all for one in layer]:
        ref[slots] = jnp.zeros((block, block), ref.dtype)
    for ref in [one for layer in b_all for one in layer]:
        ref[slots_b] = jnp.zeros((block, block), ref.dtype)
    for copy in small:
        copy.wait()
    lane = lax.broadcasted_iota(jnp.int32, (1, 128), 1)
    places = jnp.where(lane < RB * KB, slots, slots_b)
    for s in range(slots):
        places = jnp.where((lane == a_pos_s[0, s]) & (s < a_count_s[0, 0]), s, places)
    for h in range(b_pos_s.shape[0]):
        start = RB * KB + h * KB * CB
        for s in range(b_pos_s.shape[1]):
            hit = (lane == start + b_pos_s[h, s]) & (s < b_count_s[0, h])
            places = jnp.where(hit, h * b_pos_s.shape[1] + s, places)
    a_maps[0, 0] = places
    b_maps[0, 0] = places
    map_ref = a_maps.at[0, 0]
    pl.semaphore_wait(barrier, len(greeted))

    sent = []

    streams = {}

    def finish(copy, when):
        if when is None:
            copy().wait_send()
        else:
            pl.when(when)(lambda: copy().wait_send())

    def send(src, dst, s_sem, r_sem, to, when=None, stream=None):
        def copy():
            return pltpu.make_async_remote_copy(
                src_ref=src, dst_ref=dst, send_sem=s_sem, recv_sem=r_sem,
                device_id=to, device_id_type=MESH)

        flying = sent if stream is None else streams.setdefault(stream, [])
        if stream is not None and len(flying) >= IN_FLIGHT:
            finish(*flying.pop(0))
        if when is None:
            copy().start()
        else:
            pl.when(when)(lambda: copy().start())
        flying.append((copy, when))

    def arrived(dst, r_sem):
        pltpu.make_async_copy(dst, dst, r_sem).wait()

    def piece(dl, dc, q):
        return a_all[dl][dc].at[pl.ds(q * size, size)]

    def stored(dl, dr):
        return b_all[dl][dr].at[pl.ds(0, slots_b)]

    def back(dl, dc, n):
        return (n_layer - dl) % n_layer, (n - dc) % n

    for k, one in enumerate(peers):
        dl, dc = back(*one, n_col)
        send(map_ref, a_maps.at[dl, dc], am_send.at[k], am_recv.at[dl, dc], peer(*one))
    for k, one in enumerate(sides):
        dl, dr = back(*one, n_row)
        send(map_ref, b_maps.at[dl, dr], bm_send.at[k], bm_recv.at[dl, dr], side(*one))

    below, above, across = (i, c - 1, l), (i, c + 1, l), (i, c, m)
    send(b_ref, stored(1, 0), b_send.at[0], b_recv.at[1, 0], across)
    for dr in range(1, n_row):
        send(b_ref, stored(0, n_row - dr), b_send.at[dr], b_recv.at[0, n_row - dr], side(0, dr))
    for q in range(pieces):
        own = a_ref.at[pl.ds(q * size, size)]
        send(own, piece(0, n_col - 1, q), up_sem.at[0, 0, q], a_recv.at[0, n_col - 1, q], above, c + 1 < n_col, "up")
        send(own, piece(0, 1, q), down_sem.at[0, 0, q], a_recv.at[0, 1, q], below, c >= 1, "down")
        send(own, piece(1, 0, q), over_sem.at[0, 0, q], a_recv.at[1, 0, q], across, None, "over")
        if q == pieces // 2:
            arrived(stored(1, 0), b_recv.at[1, 0])
            for dr in range(1, n_row):
                send(stored(1, 0), stored(1, n_row - dr), b_pass.at[dr], b_recv.at[1, n_row - dr], side(0, dr))

    for dl, dc in peers:
        arrived(a_maps.at[dl, dc], am_recv.at[dl, dc])
    for dl, dr in sides:
        arrived(b_maps.at[dl, dr], bm_recv.at[dl, dr])
    for copy in mine:
        copy.wait()
    tables = [
        pltpu.make_async_copy(a_maps, a_places, own_sem.at[4]),
        pltpu.make_async_copy(b_maps, b_places, own_sem.at[5]),
    ]
    for copy in tables:
        copy.start()
    for copy in tables:
        copy.wait()

    def multiply(dl, dc, first=False):
        dr = dc % n_row
        a, b = a_all[dl][dc], b_all[dl][dr]
        stack = lax.div(lax.rem(i + c + dc, n_col), n_row)
        base = RB * KB + stack * KB * CB + l * width
        for k in range(KB):
            for n in range(width):
                slot = b_places[dl, dr, 0, base + k * CB + n]
                right[k * block:(k + 1) * block, n * block:(n + 1) * block] = b[slot]
        for r in range(RB):
            for k in range(KB):
                slot = a_places[dl, dc, 0, r * KB + k]
                left[r * block:(r + 1) * block, k * block:(k + 1) * block] = a[slot]
        term = jnp.dot(left[...], right[...], preferred_element_type=jnp.float32)
        if first:
            out_ref[...] = term
        else:
            out_ref[...] += term

    def at_distance(d, dl):
        def low():
            multiply(dl, n_col - d)

        def high():
            multiply(dl, d)

        def low_wait():
            for q in range(pieces):
                arrived(piece(dl, n_col - d, q), a_recv.at[dl, n_col - d, q])

        def high_wait():
            for q in range(pieces):
                arrived(piece(dl, d, q), a_recv.at[dl, d, q])

        def one(condition, wait, body):
            def run():
                @pl.when(condition)
                def _():
                    if dl:
                        wait()
                    body()
            return run

        return [one(c >= d, low_wait, low), one(c + d < n_col, high_wait, high)]

    def gram(dl):
        for dr in range(1, n_row):
            arrived(stored(dl, dr), b_recv.at[dl, dr])

    todo = [lambda: multiply(0, 0, True)]
    for d in range(1, n_col):
        for q in range(pieces):
            low, high = n_col - d, d
            over_low = c >= d
            over_high = c + d < n_col
            if d == 1 and short_cuts:
                over_low = (c >= 2) & (c < n_col - 1) if q < half else c >= 2
                over_high = (c >= 1) & (c < n_col - 2) if q < half else c < n_col - 2

            @pl.when(c >= d)
            def _():
                arrived(piece(0, low, q), a_recv.at[0, low, q])

            part = piece(0, low, q)
            if low > 1:
                send(part, piece(0, low - 1, q), up_sem.at[0, low, q], a_recv.at[0, low - 1, q], above,
                     (c >= d) & (c + 1 < n_col), "up")
            send(part, piece(1, low, q), over_sem.at[0, low, q], a_recv.at[1, low, q], across, over_low, "over low")

            @pl.when(c + d < n_col)
            def _():
                arrived(piece(0, high, q), a_recv.at[0, high, q])

            part = piece(0, high, q)
            if high + 1 < n_col:
                send(part, piece(0, high + 1, q), down_sem.at[0, high, q], a_recv.at[0, high + 1, q], below,
                     (c + d < n_col) & (c >= 1), "down")
            send(part, piece(1, high, q), over_sem.at[1, high, q], a_recv.at[1, high, q], across, over_high, "over")

            if d == 1:
                part = piece(1, 0, q)
                arrived(part, a_recv.at[1, 0, q])
                if short_cuts:
                    up = c == 0
                    down = c == n_col - 1
                    send(part, piece(1, n_col - 1, q), up_sem.at[1, 0, q], a_recv.at[1, n_col - 1, q], above, up, "turn up")
                    send(part, piece(1, 1, q), down_sem.at[1, 0, q], a_recv.at[1, 1, q], below, down, "turn down")
            if todo:
                todo.pop(0)()
        if d == n_col - 2 and short_cuts:
            for q in range(half):
                part = piece(1, 0, q)
                send(part, piece(1, n_col - 1, q), late_sem.at[0, q], a_recv.at[1, n_col - 1, q], above, c == n_col - 2, "up")
                send(part, piece(1, 1, q), late_sem.at[1, q], a_recv.at[1, 1, q], below, c == 1, "down")
                if todo:
                    todo.pop(0)()
        while todo:
            todo.pop(0)()
        todo = at_distance(d, 0)
        if d == 1:
            todo = [lambda: gram(0)] + todo + [lambda: multiply(1, 0), lambda: gram(1)]
        else:
            todo = todo + at_distance(d - 1, 1)
    todo = todo + at_distance(n_col - 1, 1)
    for one in todo:
        one()
    for flying in [sent] + list(streams.values()):
        for one in flying:
            finish(*one)


def per_device(a_vals, a_pos, a_count, b_vals, b_pos, b_count):
    n_row = lax.axis_size("row")
    n_col = lax.axis_size("col")
    n_layer = lax.axis_size("layer")
    a = a_vals[0, 0, 0]
    stacks, slots_b = b_pos.shape[-2:]
    block = a.shape[-1]
    b = b_vals[0, 0, 0].reshape(stacks * slots_b, block, block)
    pieces = max(1, 32 // n_col)
    if a.shape[0] % pieces:
        pieces = 1
    width = CB * block // n_layer
    dma = pltpu.SemaphoreType.DMA
    in_hbm = pl.BlockSpec(memory_space=pltpu.HBM)
    maps = ((n_layer, n_col, 1, 128), (n_layer, n_row, 1, 128))
    total = pl.pallas_call(
        functools.partial(kernel, n_row, n_col, n_layer, pieces),
        out_shape=jax.ShapeDtypeStruct((RB * block, width), jnp.float32),
        in_specs=[in_hbm] * 6,
        out_specs=pl.BlockSpec(memory_space=pltpu.VMEM),
        scratch_shapes=[pltpu.VMEM((a.shape[0] + 1, block, block), a.dtype)] * (n_layer * n_col)
        + [pltpu.VMEM((b.shape[0] + 1, block, block), b.dtype)] * (n_layer * n_row)
        + [
            pltpu.VMEM(maps[0], jnp.int32),
            pltpu.VMEM(maps[1], jnp.int32),
            pltpu.SMEM(maps[0], jnp.int32),
            pltpu.SMEM(maps[1], jnp.int32),
            pltpu.SMEM((1, a_pos.shape[-1]), jnp.int32),
            pltpu.SMEM((1, 1), jnp.int32),
            pltpu.SMEM((stacks, slots_b), jnp.int32),
            pltpu.SMEM((1, stacks), jnp.int32),
            pltpu.VMEM((RB * block, KB * block), a.dtype),
            pltpu.VMEM((KB * block, width), b.dtype),
            dma((n_layer, n_col, pieces)),
            dma((n_layer, n_col, pieces)),
            dma((n_layer, n_col, pieces)),
            dma((n_layer, n_col, pieces)),
            dma((n_layer * n_col,)),
            dma((n_layer, n_col)),
            dma((n_row,)),
            dma((n_row,)),
            dma((n_layer, n_row)),
            dma((n_layer * n_row,)),
            dma((n_layer, n_row)),
            dma((8,)),
            dma((2, pieces)),
        ],
        compiler_params=pltpu.CompilerParams(
            collective_id=0, has_side_effects=True, vmem_limit_bytes=63 * 1024 * 1024),
    )(a, b, a_pos[0, 0], a_count[0], b_pos[0, 0, 0], b_count[0, 0])
    return total


def solution(mesh):
    placed = (
        P("row", "col", "layer", None, None, None),
        P("row", "col", "layer", None),
        P("row", "col", "layer"),
        P("row", "col", "layer", None, None, None, None),
        P("row", "col", "layer", None, None),
        P("row", "col", "layer", None),
    )
    return jax.shard_map(
        per_device,
        mesh=mesh,
        in_specs=placed,
        out_specs=P("row", ("col", "layer")),
        check_vma=False,
    )
```

```python
import functools

import jax
import jax.numpy as jnp
from jax import lax
from jax.experimental import pallas as pl
from jax.experimental.pallas import tpu as pltpu
from jax.sharding import PartitionSpec as P

KB = 4
CB = 8
RB = 8
IN_FLIGHT = 4
MESH = pl.DeviceIdType.MESH


def kernel(n_row, n_col, n_layer, pieces,
           a_ref, b_ref, a_pos, a_count, b_pos, b_count, out_ref, *scratch):
    scratch = list(scratch)
    a_all = [[scratch.pop(0) for _ in range(n_col)] for _ in range(n_layer)]
    b_all = [[scratch.pop(0) for _ in range(n_row)] for _ in range(n_layer)]
    (a_maps, b_maps, a_places, b_places, a_pos_s, a_count_s, b_pos_s, b_count_s, left, right,
     up_sem, down_sem, over_sem, a_recv, am_send, am_recv,
     b_send, b_pass, b_recv, bm_send, bm_recv, own_sem, late_sem) = scratch
    i = lax.axis_index("row")
    c = lax.axis_index("col")
    l = lax.axis_index("layer")
    m = 1 - l
    slots = a_ref.shape[0]
    slots_b = b_ref.shape[0]
    block = a_ref.shape[-1]
    width = out_ref.shape[1] // block
    size = slots // pieces
    half = (pieces * 5 + 4) // 8
    short_cuts = n_col >= 4

    peers = [(dl, dc) for dl in range(n_layer) for dc in range(n_col) if dl or dc]
    sides = [(dl, dr) for dl in range(n_layer) for dr in range(n_row) if dl or dr]

    def peer(dl, dc):
        return (i, lax.rem(c + dc, n_col), lax.rem(l + dl, n_layer))

    def side(dl, dr):
        return (lax.rem(i + dr, n_row), c, lax.rem(l + dl, n_layer))

    barrier = pltpu.get_barrier_semaphore()
    greeted = [peer(*one) for one in peers] + [side(*one) for one in sides if one[1]]
    for one in greeted:
        pl.semaphore_signal(barrier, inc=1, device_id=one, device_id_type=MESH)
    mine = [
        pltpu.make_async_copy(a_ref, a_all[0][0].at[pl.ds(0, slots)], own_sem.at[0]),
        pltpu.make_async_copy(b_ref, b_all[0][0].at[pl.ds(0, slots_b)], own_sem.at[1]),
    ]
    small = [
        pltpu.make_async_copy(a_pos, a_pos_s, own_sem.at[2]),
        pltpu.make_async_copy(a_count, a_count_s, own_sem.at[3]),
        pltpu.make_async_copy(b_pos, b_pos_s, own_sem.at[6]),
        pltpu.make_async_copy(b_count, b_count_s, own_sem.at[7]),
    ]
    for copy in small + mine:
        copy.start()
    for ref in [one for layer in a_all for one in layer]:
        ref[slots] = jnp.zeros((block, block), ref.dtype)
    for ref in [one for layer in b_all for one in layer]:
        ref[slots_b] = jnp.zeros((block, block), ref.dtype)
    for copy in small:
        copy.wait()
    lane = lax.broadcasted_iota(jnp.int32, (1, 128), 1)
    places = jnp.where(lane < RB * KB, slots, slots_b)
    for s in range(slots):
        places = jnp.where((lane == a_pos_s[0, s]) & (s < a_count_s[0, 0]), s, places)
    for h in range(b_pos_s.shape[0]):
        start = RB * KB + h * KB * CB
        for s in range(b_pos_s.shape[1]):
            hit = (lane == start + b_pos_s[h, s]) & (s < b_count_s[0, h])
            places = jnp.where(hit, h * b_pos_s.shape[1] + s, places)
    a_maps[0, 0] = places
    b_maps[0, 0] = places
    map_ref = a_maps.at[0, 0]
    pl.semaphore_wait(barrier, len(greeted))

    sent = []

    streams = {}

    def finish(copy, when):
        if when is None:
            copy().wait_send()
        else:
            pl.when(when)(lambda: copy().wait_send())

    def send(src, dst, s_sem, r_sem, to, when=None, stream=None):
        def copy():
            return pltpu.make_async_remote_copy(
                src_ref=src, dst_ref=dst, send_sem=s_sem, recv_sem=r_sem,
                device_id=to, device_id_type=MESH)

        flying = sent if stream is None else streams.setdefault(stream, [])
        if stream is not None and len(flying) >= IN_FLIGHT:
            finish(*flying.pop(0))
        if when is None:
            copy().start()
        else:
            pl.when(when)(lambda: copy().start())
        flying.append((copy, when))

    def arrived(dst, r_sem):
        pltpu.make_async_copy(dst, dst, r_sem).wait()

    def piece(dl, dc, q):
        return a_all[dl][dc].at[pl.ds(q * size, size)]

    def stored(dl, dr):
        return b_all[dl][dr].at[pl.ds(0, slots_b)]

    def back(dl, dc, n):
        return (n_layer - dl) % n_layer, (n - dc) % n

    for k, one in enumerate(peers):
        dl, dc = back(*one, n_col)
        send(map_ref, a_maps.at[dl, dc], am_send.at[k], am_recv.at[dl, dc], peer(*one))
    for k, one in enumerate(sides):
        dl, dr = back(*one, n_row)
        send(map_ref, b_maps.at[dl, dr], bm_send.at[k], bm_recv.at[dl, dr], side(*one))

    below, above, across = (i, c - 1, l), (i, c + 1, l), (i, c, m)
    send(b_ref, stored(1, 0), b_send.at[0], b_recv.at[1, 0], across)
    for dr in range(1, n_row):
        send(b_ref, stored(0, n_row - dr), b_send.at[dr], b_recv.at[0, n_row - dr], side(0, dr))
    for q in range(pieces):
        own = a_ref.at[pl.ds(q * size, size)]
        send(own, piece(0, n_col - 1, q), up_sem.at[0, 0, q], a_recv.at[0, n_col - 1, q], above, c + 1 < n_col, "up")
        send(own, piece(0, 1, q), down_sem.at[0, 0, q], a_recv.at[0, 1, q], below, c >= 1, "down")
        send(own, piece(1, 0, q), over_sem.at[0, 0, q], a_recv.at[1, 0, q], across, None, "over")
        if q == pieces // 2:
            arrived(stored(1, 0), b_recv.at[1, 0])
            for dr in range(1, n_row):
                send(stored(1, 0), stored(1, n_row - dr), b_pass.at[dr], b_recv.at[1, n_row - dr], side(0, dr))

    for dl, dc in peers:
        arrived(a_maps.at[dl, dc], am_recv.at[dl, dc])
    for dl, dr in sides:
        arrived(b_maps.at[dl, dr], bm_recv.at[dl, dr])
    for copy in mine:
        copy.wait()
    tables = [
        pltpu.make_async_copy(a_maps, a_places, own_sem.at[4]),
        pltpu.make_async_copy(b_maps, b_places, own_sem.at[5]),
    ]
    for copy in tables:
        copy.start()
    for copy in tables:
        copy.wait()

    def multiply(dl, dc, first=False):
        dr = dc % n_row
        a, b = a_all[dl][dc], b_all[dl][dr]
        stack = lax.div(lax.rem(i + c + dc, n_col), n_row)
        base = RB * KB + stack * KB * CB + l * width
        for k in range(KB):
            for n in range(width):
                slot = b_places[dl, dr, 0, base + k * CB + n]
                right[k * block:(k + 1) * block, n * block:(n + 1) * block] = b[slot]
        for r in range(RB):
            for k in range(KB):
                slot = a_places[dl, dc, 0, r * KB + k]
                left[r * block:(r + 1) * block, k * block:(k + 1) * block] = a[slot]
        term = jnp.dot(left[...], right[...], preferred_element_type=jnp.float32)
        if first:
            out_ref[...] = term
        else:
            out_ref[...] += term

    def at_distance(d, dl):
        def low():
            multiply(dl, n_col - d)

        def high():
            multiply(dl, d)

        def low_wait():
            for q in range(pieces):
                arrived(piece(dl, n_col - d, q), a_recv.at[dl, n_col - d, q])

        def high_wait():
            for q in range(pieces):
                arrived(piece(dl, d, q), a_recv.at[dl, d, q])

        def one(condition, wait, body):
            def run():
                @pl.when(condition)
                def _():
                    if dl:
                        wait()
                    body()
            return run

        return [one(c >= d, low_wait, low), one(c + d < n_col, high_wait, high)]

    def gram(dl):
        for dr in range(1, n_row):
            arrived(stored(dl, dr), b_recv.at[dl, dr])

    todo = [lambda: multiply(0, 0, True)]
    for d in range(1, n_col):
        for q in range(pieces):
            low, high = n_col - d, d
            over_low = c >= d
            over_high = c + d < n_col
            if d == 1 and short_cuts:
                over_low = (c >= 2) & (c < n_col - 1) if q < half else c >= 2
                over_high = (c >= 1) & (c < n_col - 2) if q < half else c < n_col - 2

            @pl.when(c >= d)
            def _():
                arrived(piece(0, low, q), a_recv.at[0, low, q])

            part = piece(0, low, q)
            if low > 1:
                send(part, piece(0, low - 1, q), up_sem.at[0, low, q], a_recv.at[0, low - 1, q], above,
                     (c >= d) & (c + 1 < n_col), "up")
            send(part, piece(1, low, q), over_sem.at[0, low, q], a_recv.at[1, low, q], across, over_low, "over low")

            @pl.when(c + d < n_col)
            def _():
                arrived(piece(0, high, q), a_recv.at[0, high, q])

            part = piece(0, high, q)
            if high + 1 < n_col:
                send(part, piece(0, high + 1, q), down_sem.at[0, high, q], a_recv.at[0, high + 1, q], below,
                     (c + d < n_col) & (c >= 1), "down")
            send(part, piece(1, high, q), over_sem.at[1, high, q], a_recv.at[1, high, q], across, over_high, "over")

            if d == 1:
                part = piece(1, 0, q)
                arrived(part, a_recv.at[1, 0, q])
                if short_cuts:
                    up = c == 0
                    down = c == n_col - 1
                    send(part, piece(1, n_col - 1, q), up_sem.at[1, 0, q], a_recv.at[1, n_col - 1, q], above, up, "turn up")
                    send(part, piece(1, 1, q), down_sem.at[1, 0, q], a_recv.at[1, 1, q], below, down, "turn down")
            if todo:
                todo.pop(0)()
        if d == n_col - 2 and short_cuts:
            for q in range(half):
                part = piece(1, 0, q)
                send(part, piece(1, n_col - 1, q), late_sem.at[0, q], a_recv.at[1, n_col - 1, q], above, c == n_col - 2, "up")
                send(part, piece(1, 1, q), late_sem.at[1, q], a_recv.at[1, 1, q], below, c == 1, "down")
                if todo:
                    todo.pop(0)()
        while todo:
            todo.pop(0)()
        todo = at_distance(d, 0)
        if d == 1:
            todo = [lambda: gram(0)] + todo + [lambda: multiply(1, 0), lambda: gram(1)]
        elif d > 2:
            todo = todo + at_distance(d - 1, 1)
    for d in sorted({1, n_col - 1}):
        todo = todo + at_distance(d, 1)
    for one in todo:
        one()
    for flying in [sent] + list(streams.values()):
        for one in flying:
            finish(*one)


def per_device(a_vals, a_pos, a_count, b_vals, b_pos, b_count):
    n_row = lax.axis_size("row")
    n_col = lax.axis_size("col")
    n_layer = lax.axis_size("layer")
    a = a_vals[0, 0, 0]
    stacks, slots_b = b_pos.shape[-2:]
    block = a.shape[-1]
    b = b_vals[0, 0, 0].reshape(stacks * slots_b, block, block)
    pieces = max(1, 32 // n_col)
    if a.shape[0] % pieces:
        pieces = 1
    width = CB * block // n_layer
    dma = pltpu.SemaphoreType.DMA
    in_hbm = pl.BlockSpec(memory_space=pltpu.HBM)
    maps = ((n_layer, n_col, 1, 128), (n_layer, n_row, 1, 128))
    total = pl.pallas_call(
        functools.partial(kernel, n_row, n_col, n_layer, pieces),
        out_shape=jax.ShapeDtypeStruct((RB * block, width), jnp.float32),
        in_specs=[in_hbm] * 6,
        out_specs=pl.BlockSpec(memory_space=pltpu.VMEM),
        scratch_shapes=[pltpu.VMEM((a.shape[0] + 1, block, block), a.dtype)] * (n_layer * n_col)
        + [pltpu.VMEM((b.shape[0] + 1, block, block), b.dtype)] * (n_layer * n_row)
        + [
            pltpu.VMEM(maps[0], jnp.int32),
            pltpu.VMEM(maps[1], jnp.int32),
            pltpu.SMEM(maps[0], jnp.int32),
            pltpu.SMEM(maps[1], jnp.int32),
            pltpu.SMEM((1, a_pos.shape[-1]), jnp.int32),
            pltpu.SMEM((1, 1), jnp.int32),
            pltpu.SMEM((stacks, slots_b), jnp.int32),
            pltpu.SMEM((1, stacks), jnp.int32),
            pltpu.VMEM((RB * block, KB * block), a.dtype),
            pltpu.VMEM((KB * block, width), b.dtype),
            dma((n_layer, n_col, pieces)),
            dma((n_layer, n_col, pieces)),
            dma((n_layer, n_col, pieces)),
            dma((n_layer, n_col, pieces)),
            dma((n_layer * n_col,)),
            dma((n_layer, n_col)),
            dma((n_row,)),
            dma((n_row,)),
            dma((n_layer, n_row)),
            dma((n_layer * n_row,)),
            dma((n_layer, n_row)),
            dma((8,)),
            dma((2, pieces)),
        ],
        compiler_params=pltpu.CompilerParams(
            collective_id=0, has_side_effects=True, vmem_limit_bytes=63 * 1024 * 1024),
    )(a, b, a_pos[0, 0], a_count[0], b_pos[0, 0, 0], b_count[0, 0])
    return total


def solution(mesh):
    placed = (
        P("row", "col", "layer", None, None, None),
        P("row", "col", "layer", None),
        P("row", "col", "layer"),
        P("row", "col", "layer", None, None, None, None),
        P("row", "col", "layer", None, None),
        P("row", "col", "layer", None),
    )
    return jax.shard_map(
        per_device,
        mesh=mesh,
        in_specs=placed,
        out_specs=P("row", ("col", "layer")),
        check_vma=False,
    )
```

```python
import functools

import jax
import jax.numpy as jnp
from jax import lax
from jax.experimental import pallas as pl
from jax.experimental.pallas import tpu as pltpu
from jax.sharding import PartitionSpec as P

KB = 4
CB = 8
RB = 8
IN_FLIGHT = 4
MESH = pl.DeviceIdType.MESH


def kernel(n_row, n_col, n_layer, pieces,
           a_ref, b_ref, a_pos, a_count, b_pos, b_count, out_ref, *scratch):
    scratch = list(scratch)
    a_all = [[scratch.pop(0) for _ in range(n_col)] for _ in range(n_layer)]
    b_all = [[scratch.pop(0) for _ in range(n_row)] for _ in range(n_layer)]
    (a_maps, b_maps, a_places, b_places, a_pos_s, a_count_s, b_pos_s, b_count_s, left, right,
     up_sem, down_sem, over_sem, a_recv, am_send, am_recv,
     b_send, b_pass, b_recv, bm_send, bm_recv, own_sem, late_sem) = scratch
    i = lax.axis_index("row")
    c = lax.axis_index("col")
    l = lax.axis_index("layer")
    m = 1 - l
    slots = a_ref.shape[0]
    slots_b = b_ref.shape[0]
    block = a_ref.shape[-1]
    width = out_ref.shape[1] // block
    size = slots // pieces
    half = (pieces * 5 + 4) // 8
    short_cuts = n_col >= 4

    peers = [(dl, dc) for dl in range(n_layer) for dc in range(n_col) if dl or dc]
    sides = [(dl, dr) for dl in range(n_layer) for dr in range(n_row) if dl or dr]

    def peer(dl, dc):
        return (i, lax.rem(c + dc, n_col), lax.rem(l + dl, n_layer))

    def side(dl, dr):
        return (lax.rem(i + dr, n_row), c, lax.rem(l + dl, n_layer))

    barrier = pltpu.get_barrier_semaphore()
    greeted = [peer(*one) for one in peers] + [side(*one) for one in sides if one[1]]
    for one in greeted:
        pl.semaphore_signal(barrier, inc=1, device_id=one, device_id_type=MESH)
    mine = [
        pltpu.make_async_copy(a_ref, a_all[0][0].at[pl.ds(0, slots)], own_sem.at[0]),
        pltpu.make_async_copy(b_ref, b_all[0][0].at[pl.ds(0, slots_b)], own_sem.at[1]),
    ]
    small = [
        pltpu.make_async_copy(a_pos, a_pos_s, own_sem.at[2]),
        pltpu.make_async_copy(a_count, a_count_s, own_sem.at[3]),
        pltpu.make_async_copy(b_pos, b_pos_s, own_sem.at[6]),
        pltpu.make_async_copy(b_count, b_count_s, own_sem.at[7]),
    ]
    for copy in small + mine:
        copy.start()
    for ref in [one for layer in a_all for one in layer]:
        ref[slots] = jnp.zeros((block, block), ref.dtype)
    for ref in [one for layer in b_all for one in layer]:
        ref[slots_b] = jnp.zeros((block, block), ref.dtype)
    pl.semaphore_wait(barrier, len(greeted))

    sent = []

    streams = {}

    def finish(copy, when):
        if when is None:
            copy().wait_send()
        else:
            pl.when(when)(lambda: copy().wait_send())

    def send(src, dst, s_sem, r_sem, to, when=None, stream=None):
        def copy():
            return pltpu.make_async_remote_copy(
                src_ref=src, dst_ref=dst, send_sem=s_sem, recv_sem=r_sem,
                device_id=to, device_id_type=MESH)

        flying = sent if stream is None else streams.setdefault(stream, [])
        if stream is not None and len(flying) >= IN_FLIGHT:
            finish(*flying.pop(0))
        if when is None:
            copy().start()
        else:
            pl.when(when)(lambda: copy().start())
        flying.append((copy, when))

    def arrived(dst, r_sem):
        pltpu.make_async_copy(dst, dst, r_sem).wait()

    def piece(dl, dc, q):
        return a_all[dl][dc].at[pl.ds(q * size, size)]

    def stored(dl, dr):
        return b_all[dl][dr].at[pl.ds(0, slots_b)]

    def back(dl, dc, n):
        return (n_layer - dl) % n_layer, (n - dc) % n

    below, above, across = (i, c - 1, l), (i, c + 1, l), (i, c, m)

    def own_piece(q):
        own = a_ref.at[pl.ds(q * size, size)]
        send(own, piece(0, n_col - 1, q), up_sem.at[0, 0, q], a_recv.at[0, n_col - 1, q], above, c + 1 < n_col, "up")
        send(own, piece(0, 1, q), down_sem.at[0, 0, q], a_recv.at[0, 1, q], below, c >= 1, "down")
        send(own, piece(1, 0, q), over_sem.at[0, 0, q], a_recv.at[1, 0, q], across, None, "over")

    first = min(IN_FLIGHT, pieces)
    for q in range(first):
        own_piece(q)
    send(b_ref, stored(1, 0), b_send.at[0], b_recv.at[1, 0], across)
    for copy in small:
        copy.wait()
    lane = lax.broadcasted_iota(jnp.int32, (1, 128), 1)
    places = jnp.where(lane < RB * KB, slots, slots_b)
    for s in range(slots):
        places = jnp.where((lane == a_pos_s[0, s]) & (s < a_count_s[0, 0]), s, places)
    for h in range(b_pos_s.shape[0]):
        start = RB * KB + h * KB * CB
        for s in range(b_pos_s.shape[1]):
            hit = (lane == start + b_pos_s[h, s]) & (s < b_count_s[0, h])
            places = jnp.where(hit, h * b_pos_s.shape[1] + s, places)
    a_maps[0, 0] = places
    b_maps[0, 0] = places
    map_ref = a_maps.at[0, 0]
    for k, one in enumerate(peers):
        dl, dc = back(*one, n_col)
        send(map_ref, a_maps.at[dl, dc], am_send.at[k], am_recv.at[dl, dc], peer(*one))
    for k, one in enumerate(sides):
        dl, dr = back(*one, n_row)
        send(map_ref, b_maps.at[dl, dr], bm_send.at[k], bm_recv.at[dl, dr], side(*one))

    for dr in range(1, n_row):
        send(b_ref, stored(0, n_row - dr), b_send.at[dr], b_recv.at[0, n_row - dr], side(0, dr))
    for q in range(first, pieces):
        own_piece(q)
    arrived(stored(1, 0), b_recv.at[1, 0])
    for dr in range(1, n_row):
        send(stored(1, 0), stored(1, n_row - dr), b_pass.at[dr], b_recv.at[1, n_row - dr], side(0, dr))

    for dl, dc in peers:
        arrived(a_maps.at[dl, dc], am_recv.at[dl, dc])
    for dl, dr in sides:
        arrived(b_maps.at[dl, dr], bm_recv.at[dl, dr])
    for copy in mine:
        copy.wait()
    tables = [
        pltpu.make_async_copy(a_maps, a_places, own_sem.at[4]),
        pltpu.make_async_copy(b_maps, b_places, own_sem.at[5]),
    ]
    for copy in tables:
        copy.start()
    for copy in tables:
        copy.wait()

    def multiply(dl, dc, first=False):
        dr = dc % n_row
        a, b = a_all[dl][dc], b_all[dl][dr]
        stack = lax.div(lax.rem(i + c + dc, n_col), n_row)
        base = RB * KB + stack * KB * CB + l * width
        for k in range(KB):
            for n in range(width):
                slot = b_places[dl, dr, 0, base + k * CB + n]
                right[k * block:(k + 1) * block, n * block:(n + 1) * block] = b[slot]
        for r in range(RB):
            for k in range(KB):
                slot = a_places[dl, dc, 0, r * KB + k]
                left[r * block:(r + 1) * block, k * block:(k + 1) * block] = a[slot]
        term = jnp.dot(left[...], right[...], preferred_element_type=jnp.float32)
        if first:
            out_ref[...] = term
        else:
            out_ref[...] += term

    def at_distance(d, dl):
        def low():
            multiply(dl, n_col - d)

        def high():
            multiply(dl, d)

        def low_wait():
            for q in range(pieces):
                arrived(piece(dl, n_col - d, q), a_recv.at[dl, n_col - d, q])

        def high_wait():
            for q in range(pieces):
                arrived(piece(dl, d, q), a_recv.at[dl, d, q])

        def one(condition, wait, body):
            def run():
                @pl.when(condition)
                def _():
                    if dl:
                        wait()
                    body()
            return run

        return [one(c >= d, low_wait, low), one(c + d < n_col, high_wait, high)]

    def gram(dl):
        for dr in range(1, n_row):
            arrived(stored(dl, dr), b_recv.at[dl, dr])

    todo = [lambda: multiply(0, 0, True)]
    for d in range(1, n_col):
        for q in range(pieces):
            low, high = n_col - d, d
            over_low = c >= d
            over_high = c + d < n_col
            if d == 1 and short_cuts:
                over_low = (c >= 2) & (c < n_col - 1) if q < half else c >= 2
                over_high = (c >= 1) & (c < n_col - 2) if q < half else c < n_col - 2

            @pl.when(c >= d)
            def _():
                arrived(piece(0, low, q), a_recv.at[0, low, q])

            part = piece(0, low, q)
            if low > 1:
                send(part, piece(0, low - 1, q), up_sem.at[0, low, q], a_recv.at[0, low - 1, q], above,
                     (c >= d) & (c + 1 < n_col), "up")
            send(part, piece(1, low, q), over_sem.at[0, low, q], a_recv.at[1, low, q], across, over_low, "over low")

            @pl.when(c + d < n_col)
            def _():
                arrived(piece(0, high, q), a_recv.at[0, high, q])

            part = piece(0, high, q)
            if high + 1 < n_col:
                send(part, piece(0, high + 1, q), down_sem.at[0, high, q], a_recv.at[0, high + 1, q], below,
                     (c + d < n_col) & (c >= 1), "down")
            send(part, piece(1, high, q), over_sem.at[1, high, q], a_recv.at[1, high, q], across, over_high, "over")

            if d == 1:
                part = piece(1, 0, q)
                arrived(part, a_recv.at[1, 0, q])
                if short_cuts:
                    up = c == 0
                    down = c == n_col - 1
                    send(part, piece(1, n_col - 1, q), up_sem.at[1, 0, q], a_recv.at[1, n_col - 1, q], above, up, "turn up")
                    send(part, piece(1, 1, q), down_sem.at[1, 0, q], a_recv.at[1, 1, q], below, down, "turn down")
            if todo:
                todo.pop(0)()
        if d == n_col - 2 and short_cuts:
            for q in range(half):
                part = piece(1, 0, q)
                send(part, piece(1, n_col - 1, q), late_sem.at[0, q], a_recv.at[1, n_col - 1, q], above, c == n_col - 2, "up")
                send(part, piece(1, 1, q), late_sem.at[1, q], a_recv.at[1, 1, q], below, c == 1, "down")
                if todo:
                    todo.pop(0)()
        while todo:
            todo.pop(0)()
        todo = at_distance(d, 0)
        if d == 1:
            todo = [lambda: gram(0)] + todo + [lambda: multiply(1, 0), lambda: gram(1)]
        elif d > 2:
            todo = todo + at_distance(d - 1, 1)
    for d in sorted({1, n_col - 1}):
        todo = todo + at_distance(d, 1)
    for one in todo:
        one()
    for flying in [sent] + list(streams.values()):
        for one in flying:
            finish(*one)


def per_device(a_vals, a_pos, a_count, b_vals, b_pos, b_count):
    n_row = lax.axis_size("row")
    n_col = lax.axis_size("col")
    n_layer = lax.axis_size("layer")
    a = a_vals[0, 0, 0]
    stacks, slots_b = b_pos.shape[-2:]
    block = a.shape[-1]
    b = b_vals[0, 0, 0].reshape(stacks * slots_b, block, block)
    pieces = max(1, 32 // n_col)
    if a.shape[0] % pieces:
        pieces = 1
    width = CB * block // n_layer
    dma = pltpu.SemaphoreType.DMA
    in_hbm = pl.BlockSpec(memory_space=pltpu.HBM)
    maps = ((n_layer, n_col, 1, 128), (n_layer, n_row, 1, 128))
    total = pl.pallas_call(
        functools.partial(kernel, n_row, n_col, n_layer, pieces),
        out_shape=jax.ShapeDtypeStruct((RB * block, width), jnp.float32),
        in_specs=[in_hbm] * 6,
        out_specs=pl.BlockSpec(memory_space=pltpu.VMEM),
        scratch_shapes=[pltpu.VMEM((a.shape[0] + 1, block, block), a.dtype)] * (n_layer * n_col)
        + [pltpu.VMEM((b.shape[0] + 1, block, block), b.dtype)] * (n_layer * n_row)
        + [
            pltpu.VMEM(maps[0], jnp.int32),
            pltpu.VMEM(maps[1], jnp.int32),
            pltpu.SMEM(maps[0], jnp.int32),
            pltpu.SMEM(maps[1], jnp.int32),
            pltpu.SMEM((1, a_pos.shape[-1]), jnp.int32),
            pltpu.SMEM((1, 1), jnp.int32),
            pltpu.SMEM((stacks, slots_b), jnp.int32),
            pltpu.SMEM((1, stacks), jnp.int32),
            pltpu.VMEM((RB * block, KB * block), a.dtype),
            pltpu.VMEM((KB * block, width), b.dtype),
            dma((n_layer, n_col, pieces)),
            dma((n_layer, n_col, pieces)),
            dma((n_layer, n_col, pieces)),
            dma((n_layer, n_col, pieces)),
            dma((n_layer * n_col,)),
            dma((n_layer, n_col)),
            dma((n_row,)),
            dma((n_row,)),
            dma((n_layer, n_row)),
            dma((n_layer * n_row,)),
            dma((n_layer, n_row)),
            dma((8,)),
            dma((2, pieces)),
        ],
        compiler_params=pltpu.CompilerParams(
            collective_id=0, has_side_effects=True, vmem_limit_bytes=63 * 1024 * 1024),
    )(a, b, a_pos[0, 0], a_count[0], b_pos[0, 0, 0], b_count[0, 0])
    return total


def solution(mesh):
    placed = (
        P("row", "col", "layer", None, None, None),
        P("row", "col", "layer", None),
        P("row", "col", "layer"),
        P("row", "col", "layer", None, None, None, None),
        P("row", "col", "layer", None, None),
        P("row", "col", "layer", None),
    )
    return jax.shard_map(
        per_device,
        mesh=mesh,
        in_specs=placed,
        out_specs=P("row", ("col", "layer")),
        check_vma=False,
    )
```
